32 devices in a mesh: groups: 2 (over y), hist: 4 (over z), tower: 2 (over x), head: 2 (over core).
Axes of the slice: x: 2, y: 2, z: 4, core: 2. Of those that a mesh axis runs over, the one named last changes fastest.
Arguments:
- queries: bfloat16 [1024, 1024], P(('groups', 'hist', 'tower'), 'head'), parts along dimension 0, may hold values from -6 to 6
- hist_keys: bfloat16 [4, 1024, 1024], P('groups', 'hist', 'head'), parts along dimension 0, may hold values from -6 to 6
- hist_values: bfloat16 [4, 1024, 1024], P('groups', 'hist', 'head'), parts along dimension 0, may hold values from -6 to 6
- cand_user: int32 [1024], P(('groups', 'hist', 'tower')), parts along dimension 0, may hold values from 0 to 1
- time_bucket: int32 [4, 1024], P('groups', 'hist'), parts along dimension 0, may hold values from 0 to 127
- hist_len: int32 [4], P('groups'), parts along dimension 0, may hold values from 256 to 1024
- cand_gate: bfloat16 [1024, 1024], P(('groups', 'hist', 'tower'), 'head'), parts along dimension 0, may hold values from -6 to 6
- time_bias: float32 [128, 8], P(None, 'head'), may hold values from -4 to 4
- tower_in: bfloat16 [1024, 4096], P('head', 'tower'), may hold values from -0.1875 to 0.1875
- tower_bias: float32 [4096], P('tower'), may hold values from -4 to 4
- tower_out: float32 [4096], P('tower'), may hold values from -0.09375 to 0.09375
Outputs:
- cand_states: bfloat16 [1024, 1024], P(('groups', 'hist', 'tower'), 'head'), parts along dimension 0
- cand_scores: float32 [1024], P(('groups', 'hist', 'tower')), parts along dimension 0
The draws below stay inside these ranges and needn't reach their ends.
There are 2 independent parts, one for each index of `groups`. The reference program is written for one: setup_inputs(seed, part) draws one part's arguments, and reference() takes and returns one part's arrays. A program takes and returns all parts, laid end to end along the dimension named above; an argument that names none is the same for every part. Nothing has to cross between parts.
All inputs are finite; a program needn't handle non-finite values.
Results may differ from the reference program's by a relative error of at most 0.017.
Values may be sent and summed in bfloat16 or wider, within the bound.
No kernel may reach another device: no remote copies, remote signals or barrier semaphores. Data moves between devices by JAX's collectives and lax.ppermute only.
A program may use at most 64 MiB of HBM per device.

```python
import jax
import jax.numpy as jnp
from jax import lax

D = 1024
H = 8
DH = 128
FF = 4096
NB = 128
USERS = 2
HL_DEV = 256
HLEN = 1024
CANDS = 512
N_HIST = 4


def set_ends(entries, stream_key, low, largest):
    longest = entries.shape.index(max(entries.shape))
    spots = []
    for shift in (0, 1):
        where = [jax.random.randint(jax.random.fold_in(stream_key, axis), (), 0, length) for axis, length in enumerate(entries.shape)]
        where[longest] = (where[longest] + shift) % entries.shape[longest]
        spots.append(tuple(where))
    return entries.at[spots[0]].set(low).at[spots[1]].set(largest)


def steps_of(rng, dims, pieces, least, top_value):
    level, own = 1.0, jax.random.fold_in(rng, 6)
    for position, shards_of in pieces:
        steps = jnp.exp(jax.random.uniform(jax.random.fold_in(own, position), (shards_of,), jnp.float32, least / len(pieces), top_value / len(pieces)))
        level = level * jnp.repeat(steps, dims[position] // shards_of).reshape([-1 if axis == position else 1 for axis in range(len(dims))])
    return level


def centred(own_key, shape, scale, reach, pieces=(), kind=jnp.bfloat16):
    drawn = jax.random.normal(own_key, shape, jnp.float32) * scale
    if len(pieces) > 0:
        drawn = steps_of(own_key, shape, pieces, -0.22, 0.18) * drawn
    return jnp.clip(drawn, min=-reach, max=reach).astype(kind)


def setup_inputs(seed: int = 0, part: int = 0) -> dict:
    keys = jax.random.split(jax.random.key(seed), 12)
    part_splits = jax.random.split(jax.random.fold_in(keys[11], part), 12)
    return {
        "queries": centred(part_splits[0], (CANDS, D), 1.0, 6.0, ((0, 8), (1, 2))),
        "hist_keys": centred(part_splits[1], (USERS, HLEN, D), 1.0, 6.0, ((1, 4), (2, 2))),
        "hist_values": centred(part_splits[2], (USERS, HLEN, D), 1.0, 6.0, ((1, 4), (2, 2))),
        "cand_user": set_ends(jax.random.randint(part_splits[3], (CANDS,), 0, USERS), jax.random.fold_in(part_splits[3], 1), 0, USERS - 1).astype(jnp.int32),
        "time_bucket": set_ends(jax.random.randint(part_splits[4], (USERS, HLEN), 0, NB), jax.random.fold_in(part_splits[4], 1), 0, NB - 1).astype(jnp.int32),
        "hist_len": jax.random.randint(part_splits[5], (USERS,), HLEN // 4, HLEN + 1).astype(jnp.int32),
        "cand_gate": centred(part_splits[6], (CANDS, D), 1.0, 6.0, ((0, 8), (1, 2))),
        "time_bias": centred(keys[7], (NB, H), 1.0, 4.0, ((1, 2),), jnp.float32),
        "tower_in": centred(keys[8], (D, FF), D ** -0.5, 0.1875, ((0, 2), (1, 2))),
        "tower_bias": centred(keys[9], (FF,), 1.0, 4.0, ((0, 2),), jnp.float32),
        "tower_out": centred(keys[10], (FF,), FF ** -0.5, 0.09375, ((0, 2),), jnp.float32),
    }


def reference(queries, hist_keys, hist_values, cand_user, time_bucket, hist_len, cand_gate, time_bias, tower_in, tower_bias, tower_out):
    score_scale = DH ** (-0.5)
    positions = jnp.arange(HLEN, dtype=jnp.int32)
    key_live = positions[None, :] < hist_len[:, None]
    event_bias = time_bias[time_bucket]
    user_ids = jnp.arange(USERS, dtype=jnp.int32)
    shard_keys = jnp.swapaxes(hist_keys.reshape(USERS, N_HIST, HL_DEV, D), 0, 1)
    shard_values = jnp.swapaxes(hist_values.reshape(USERS, N_HIST, HL_DEV, D), 0, 1)
    shard_bias = jnp.swapaxes(event_bias.reshape(USERS, N_HIST, HL_DEV, H), 0, 1)
    shard_live = jnp.swapaxes(key_live.reshape(USERS, N_HIST, HL_DEV), 0, 1)

    def one_user(total, inputs):
        user_keys, user_values, user_bias, user_live, user_id = inputs
        same_user = jnp.where((cand_user == user_id)[:, None] & user_live[None, :], 1.0, 0.0).astype(jnp.float32)
        head_outputs = []
        for head_index in range(H):
            first = head_index * DH
            logits = lax.dot_general(queries[:, first:first + DH], user_keys[:, first:first + DH], (((1,), (1,)), ((), ())), preferred_element_type=jnp.float32)
            logits = logits * score_scale + user_bias[:, head_index][None, :]
            weights_bf = (jax.nn.silu(logits) * same_user).astype(jnp.bfloat16)
            head_outputs.append(jnp.dot(weights_bf, user_values[:, first:first + DH], preferred_element_type=jnp.float32))
        return (total + jnp.concatenate(head_outputs, axis=1), None)

    def one_shard(total, inputs):
        keys_s, values_s, bias_s, live_s = inputs
        start_share = jnp.zeros((CANDS, D), jnp.float32)
        share, unused_inner = lax.scan(one_user, start_share, (keys_s, values_s, bias_s, live_s, user_ids))
        rounded = lax.optimization_barrier(share.astype(jnp.bfloat16))
        return (total + rounded.astype(jnp.float32), None)
    start_total = jnp.zeros((CANDS, D), jnp.float32)
    attended, unused = lax.scan(one_shard, start_total, (shard_keys, shard_values, shard_bias, shard_live))
    row_mean = lax.optimization_barrier(jnp.sum(attended, axis=1)) / D
    row_var = lax.optimization_barrier(jnp.sum(attended * attended, axis=1)) / D - row_mean * row_mean
    cand_states = ((attended - row_mean[:, None]) * lax.rsqrt(row_var[:, None] + 1e-05) * cand_gate.astype(jnp.float32)).astype(jnp.bfloat16)
    pre_act = jnp.dot(cand_states, tower_in, preferred_element_type=jnp.float32) + tower_bias[None, :]
    hidden = jax.nn.silu(pre_act)
    cand_scores = jnp.dot(hidden, tower_out, precision=lax.Precision.HIGHEST)
    return (cand_states, cand_scores)
```

```python
import functools

import jax
import jax.numpy as jnp
from jax import lax
from jax.experimental import pallas as pl
from jax.experimental.pallas import tpu as pltpu
from jax.sharding import PartitionSpec as P

DH = 128
LANES = 128
DEAD = -1e30
VMEM = pl.BlockSpec(memory_space=pltpu.VMEM)
SMEM = pl.BlockSpec(memory_space=pltpu.SMEM)
LIMIT = 32 * 1024 * 1024


def partner(index, step, count):
    if count & (count - 1) == 0:
        return index ^ step
    return (index + step) % count


def fetch(x, axis, step, count):
    return lax.ppermute(x, axis, [(partner(i, step, count), i) for i in range(count)])


def give(x, axis, step, count):
    return lax.ppermute(x, axis, [(i, partner(i, step, count)) for i in range(count)])


def call(body, outs, specs, flops, nbytes):
    return pl.pallas_call(
        body,
        out_shape=outs,
        in_specs=specs,
        out_specs=jax.tree.map(lambda _: VMEM, outs),
        compiler_params=pltpu.CompilerParams(vmem_limit_bytes=LIMIT),
        cost_estimate=pl.CostEstimate(
            flops=flops, bytes_accessed=nbytes, transcendentals=0
        ),
    )


def bias_body(len_ref, bucket_ref, table_ref, out_ref):
    users, events = bucket_ref.shape
    heads, buckets = table_ref.shape
    table = table_ref[...] * 0.5
    high = table.astype(jnp.bfloat16)
    rest = table - high.astype(jnp.float32)
    middle = rest.astype(jnp.bfloat16)
    low = (rest - middle.astype(jnp.float32)).astype(jnp.bfloat16)
    position = lax.axis_index("hist") * events + lax.broadcasted_iota(
        jnp.int32, (heads, events), 1
    )
    bucket_ids = lax.broadcasted_iota(jnp.int32, (buckets, events), 0)
    for user in range(users):
        onehot = jnp.where(bucket_ids == bucket_ref[user : user + 1, :], 1.0, 0.0).astype(
            jnp.bfloat16
        )
        bias = sum(
            jnp.dot(piece, onehot, preferred_element_type=jnp.float32)
            for piece in (high, middle, low)
        )
        out_ref[user * heads : (user + 1) * heads, :] = jnp.where(
            position < len_ref[user], bias, DEAD
        )


def share_body(q_ref, id_ref, k_ref, v_ref, bias_ref, out_ref):
    users, events, width = k_ref.shape
    count = q_ref.shape[0]
    heads = width // DH
    half_scale = 0.5 * DH ** (-0.5)
    ids = jnp.broadcast_to(id_ref[...].astype(jnp.float32), (8, count)).astype(jnp.bfloat16)
    eighth = jnp.full((8, LANES), 0.125, jnp.bfloat16)
    owner = lax.dot_general(
        ids, eighth, (((0,), (0,)), ((), ())), preferred_element_type=jnp.float32
    )
    mine = [owner == float(user) for user in range(users)]
    wide = [
        jnp.concatenate([owner] * (events // LANES), axis=1) == float(user)
        for user in range(users)
    ]
    for head in range(heads):
        cols = slice(head * DH, (head + 1) * DH)
        query = q_ref[:, cols].astype(jnp.float32)
        query = jnp.concatenate(
            [jnp.where(mask, query, 0.0).astype(jnp.bfloat16) for mask in mine], axis=1
        )
        keys = jnp.concatenate([k_ref[user, :, cols] for user in range(users)], axis=1)
        logits = lax.dot_general(
            query, keys, (((1,), (1,)), ((), ())), preferred_element_type=jnp.float32
        )
        bias = jnp.broadcast_to(bias_ref[head : head + 1, :], (count, events))
        for user in range(1, users):
            row = user * heads + head
            bias = jnp.where(wide[user], bias_ref[row : row + 1, :], bias)
        half = logits * half_scale + bias
        weight = (half * jnp.tanh(half) + half).astype(jnp.bfloat16)
        values = jnp.concatenate([v_ref[user, :, cols] for user in range(users)], axis=1)
        mixed = jnp.dot(weight, values, preferred_element_type=jnp.float32)
        share = mixed[:, :DH]
        for user in range(1, users):
            share = jnp.where(mine[user], mixed[:, user * DH : (user + 1) * DH], share)
        out_ref[:, cols] = share.astype(jnp.bfloat16)


def total_body(*refs):
    *share_refs, total_ref, stats_ref = refs
    total = share_refs[0][...].astype(jnp.float32)
    for share_ref in share_refs[1:]:
        total = total + share_ref[...].astype(jnp.float32)
    total_ref[...] = total
    row_sum = jnp.sum(total, axis=1, keepdims=True)
    row_squares = jnp.sum(total * total, axis=1, keepdims=True)
    lane = lax.broadcasted_iota(jnp.int32, stats_ref.shape, 1)
    stats_ref[...] = jnp.where(lane < LANES // 2, row_sum, row_squares)


def states_body(features, total_ref, *refs):
    *stats_refs, gate_ref, out_ref = refs
    stats = stats_refs[0][...]
    for stats_ref in stats_refs[1:]:
        stats = stats + stats_ref[...]
    mean = stats[:, 0:1] / features
    variance = stats[:, LANES // 2 : LANES // 2 + 1] / features - mean * mean
    out_ref[...] = (
        (total_ref[...] - mean)
        * lax.rsqrt(variance + 1e-05)
        * gate_ref[...].astype(jnp.float32)
    ).astype(jnp.bfloat16)


def tower_body(blocks, sides, *refs):
    rows = [
        jnp.concatenate([refs[side * blocks + b][...] for b in range(blocks)], axis=0)
        for side in range(sides)
    ]
    refs = refs[blocks * sides :]
    own_ref, other_refs = refs[0], refs[1:sides]
    bias_ref, out_w_ref = refs[sides], refs[sides + 1]
    score_refs = refs[sides + 2 :]
    count = rows[0].shape[0]
    units = own_ref.shape[1] // sides
    step = min(256, units)
    start = lax.axis_index("head") * units
    total = jnp.zeros((count, LANES), jnp.float32)
    for first in range(0, units, step):
        cols = pl.ds(pl.multiple_of(start + first, LANES), step)
        act = jnp.dot(rows[0], own_ref[:, cols], preferred_element_type=jnp.float32)
        for side in range(1, sides):
            act = act + jnp.dot(
                rows[side],
                other_refs[side - 1][:, first : first + step],
                preferred_element_type=jnp.float32,
            )
        half = 0.5 * (act + bias_ref[:, cols])
        hidden = half * jnp.tanh(half) + half
        part = hidden * out_w_ref[:, cols]
        for lane in range(0, step, LANES):
            total = total + part[:, lane : lane + LANES]
    scores = jnp.sum(total.T, axis=0, keepdims=True)
    each = count // blocks
    for b in range(blocks):
        score_refs[b][...] = scores[:, b * each : (b + 1) * each]


def local(
    sizes,
    queries,
    hist_keys,
    hist_values,
    cand_user,
    time_bucket,
    hist_len,
    cand_gate,
    time_bias,
    tower_in,
    tower_bias,
    tower_out,
):
    hists, towers, sides = sizes["hist"], sizes["tower"], sizes["head"]
    users, events, width = hist_keys.shape
    count = queries.shape[0]
    heads = width // DH
    features = width * sides
    f32, bf16 = jnp.float32, jnp.bfloat16

    ids = cand_user.reshape(1, count)
    blocks = [(queries, ids)] + [
        (fetch(queries, "hist", step, hists), fetch(ids, "hist", step, hists))
        for step in range(1, hists)
    ]

    units = tower_in.shape[1] // sides
    side = lax.axis_index("head")
    others = []
    for step in range(1, sides):
        wanted = partner(side, step, sides)
        piece = lax.dynamic_slice_in_dim(tower_in, wanted * units, units, axis=1)
        others.append(give(piece, "head", step, sides))

    bias = call(
        bias_body,
        jax.ShapeDtypeStruct((users * heads, events), f32),
        [SMEM, VMEM, VMEM],
        users * heads * events * time_bias.shape[0] * 6,
        users * heads * events * 4,
    )(hist_len, time_bucket, time_bias.T)

    share_call = call(
        share_body,
        jax.ShapeDtypeStruct((count, width), bf16),
        [VMEM] * 5,
        4 * count * users * events * width,
        4 * users * events * width,
    )
    shares = []
    for step, (query, owner) in enumerate(blocks):
        share = share_call(query, owner, hist_keys, hist_values, bias)
        shares.append(share if step == 0 else give(share, "hist", step, hists))

    total, stats = call(
        total_body,
        (
            jax.ShapeDtypeStruct((count, width), f32),
            jax.ShapeDtypeStruct((count, LANES), f32),
        ),
        [VMEM] * hists,
        8 * count * width,
        8 * count * width,
    )(*shares)
    side_stats = [stats] + [fetch(stats, "head", step, sides) for step in range(1, sides)]
    cand_states = call(
        functools.partial(states_body, features),
        jax.ShapeDtypeStruct((count, width), bf16),
        [VMEM] * (2 + sides),
        8 * count * width,
        8 * count * width,
    )(total, *side_stats, cand_gate)

    def reach(x, tower_step, side_step, move):
        if tower_step == 0 and side_step == 0:
            return x
        pairs = []
        for t in range(towers):
            for s in range(sides):
                here = t * sides + s
                there = partner(t, tower_step, towers) * sides + partner(s, side_step, sides)
                pairs.append((there, here) if move == "fetch" else (here, there))
        return lax.ppermute(x, ("tower", "head"), pairs)

    rows = [
        reach(cand_states, tower_step, side_step, "fetch")
        for side_step in range(sides)
        for tower_step in range(towers)
    ]
    scores = call(
        functools.partial(tower_body, towers, sides),
        tuple(jax.ShapeDtypeStruct((1, count), f32) for _ in range(towers)),
        [VMEM] * (towers * sides + sides + 2),
        2 * towers * count * features * units,
        2 * features * units,
    )(*rows, tower_in, *others, tower_bias.reshape(1, -1), tower_out.reshape(1, -1))
    cand_scores = None
    for tower_step in range(towers):
        part = reach(scores[tower_step], tower_step, 0, "give")
        for side_step in range(1, sides):
            part = part + reach(scores[tower_step], tower_step, side_step, "give")
        cand_scores = part if cand_scores is None else cand_scores + part
    return (cand_states, cand_scores.reshape(count))


def solution(mesh):
    return jax.shard_map(
        functools.partial(local, dict(mesh.shape)),
        mesh=mesh,
        in_specs=(
            P(("groups", "hist", "tower"), "head"),
            P("groups", "hist", "head"),
            P("groups", "hist", "head"),
            P(("groups", "hist", "tower")),
            P("groups", "hist"),
            P("groups"),
            P(("groups", "hist", "tower"), "head"),
            P(None, "head"),
            P("head", "tower"),
            P("tower"),
            P("tower"),
        ),
        out_specs=(P(("groups", "hist", "tower"), "head"), P(("groups", "hist", "tower"))),
        check_vma=False,
    )
```

```python
import functools

import jax
import jax.numpy as jnp
from jax import lax
from jax.experimental import pallas as pl
from jax.experimental.pallas import tpu as pltpu
from jax.sharding import PartitionSpec as P

DH = 128
LANES = 128
DEAD = -1e30
HBM = pl.BlockSpec(memory_space=pltpu.HBM)
VMEM = pl.BlockSpec(memory_space=pltpu.VMEM)
SMEM = pl.BlockSpec(memory_space=pltpu.SMEM)
LIMIT = 32 * 1024 * 1024
BIASCOST = 1000000000
SHARECOST = 16


def GROUPS(remote):
    return [remote[-1:], remote[:-1]]


def partner(index, step, count):
    if count & (count - 1) == 0:
        return index ^ step
    return (index + step) % count


def fetch(x, axis, step, count):
    return lax.ppermute(x, axis, [(partner(i, step, count), i) for i in range(count)])


def give(x, axis, step, count):
    return lax.ppermute(x, axis, [(i, partner(i, step, count)) for i in range(count)])


def call(body, outs, specs, flops, nbytes, out_specs=None, scratch=(), limit=LIMIT):
    return pl.pallas_call(
        body,
        out_shape=outs,
        in_specs=specs,
        out_specs=out_specs or jax.tree.map(lambda _: VMEM, outs),
        scratch_shapes=scratch,
        compiler_params=pltpu.CompilerParams(vmem_limit_bytes=limit),
        cost_estimate=pl.CostEstimate(
            flops=flops, bytes_accessed=nbytes, transcendentals=0
        ),
    )


def bias_body(len_ref, bucket_ref, table_ref, out_ref):
    users, events = bucket_ref.shape
    heads, buckets = table_ref.shape
    table = table_ref[...] * 0.5
    high = table.astype(jnp.bfloat16)
    rest = table - high.astype(jnp.float32)
    middle = rest.astype(jnp.bfloat16)
    low = (rest - middle.astype(jnp.float32)).astype(jnp.bfloat16)
    position = lax.axis_index("hist") * events + lax.broadcasted_iota(
        jnp.int32, (heads, events), 1
    )
    bucket_ids = lax.broadcasted_iota(jnp.int32, (buckets, events), 0)
    for user in range(users):
        onehot = jnp.where(bucket_ids == bucket_ref[user : user + 1, :], 1.0, 0.0).astype(
            jnp.bfloat16
        )
        bias = sum(
            jnp.dot(piece, onehot, preferred_element_type=jnp.float32)
            for piece in (high, middle, low)
        )
        out_ref[user * heads : (user + 1) * heads, :] = jnp.where(
            position < len_ref[user], bias, DEAD
        )


def share_body(blocks, *refs):
    packed_refs, (k_ref, v_ref, bias_ref), out_refs = (
        refs[:blocks],
        refs[blocks : blocks + 3],
        refs[blocks + 3 :],
    )
    users, events, width = k_ref.shape
    each = out_refs[0].shape[0]
    heads = width // DH
    half_scale = 0.5 * DH ** (-0.5)
    ones = jnp.ones((8, LANES), jnp.bfloat16)
    owner = jnp.concatenate(
        [
            lax.dot_general(
                ref[each:, :LANES],
                ones,
                (((0,), (0,)), ((), ())),
                preferred_element_type=jnp.float32,
            )[:each]
            for ref in packed_refs
        ],
        axis=0,
    )
    mine = [owner == float(user) for user in range(users)]
    wide = [
        jnp.concatenate([owner] * (events // LANES), axis=1) == float(user)
        for user in range(users)
    ]
    for head in range(heads):
        cols = slice(head * DH, (head + 1) * DH)
        query = jnp.concatenate([ref[:each, cols] for ref in packed_refs], axis=0)
        query = query.astype(jnp.float32)
        query = jnp.concatenate(
            [jnp.where(mask, query, 0.0).astype(jnp.bfloat16) for mask in mine], axis=1
        )
        keys = jnp.concatenate([k_ref[user, :, cols] for user in range(users)], axis=1)
        logits = lax.dot_general(
            query, keys, (((1,), (1,)), ((), ())), preferred_element_type=jnp.float32
        )
        bias = jnp.broadcast_to(bias_ref[head : head + 1, :], logits.shape)
        for user in range(1, users):
            row = user * heads + head
            bias = jnp.where(wide[user], bias_ref[row : row + 1, :], bias)
        half = logits * half_scale + bias
        weight = (half * jnp.tanh(half) + half).astype(jnp.bfloat16)
        values = jnp.concatenate([v_ref[user, :, cols] for user in range(users)], axis=1)
        mixed = jnp.dot(weight, values, preferred_element_type=jnp.float32)
        share = mixed[:, :DH]
        for user in range(1, users):
            share = jnp.where(mine[user], mixed[:, user * DH : (user + 1) * DH], share)
        share = share.astype(jnp.bfloat16)
        for block, out_ref in enumerate(out_refs):
            out_ref[:, cols] = share[block * each : (block + 1) * each]


def total_body(*refs):
    *share_refs, total_ref, sent_ref = refs
    total = share_refs[0][...].astype(jnp.float32)
    for share_ref in share_refs[1:]:
        total = total + share_ref[...].astype(jnp.float32)
    total_ref[...] = total
    sent_ref[...] = total.astype(jnp.bfloat16)


def tower_body(blocks, sides, *refs):
    parts = blocks * sides
    rows_refs, gate_refs, refs = refs[:parts], refs[parts : 2 * parts], refs[2 * parts :]
    weight_refs = refs[:sides]
    bias_ref, out_w_ref = refs[sides], refs[sides + 1]
    states_ref, *score_refs, own_buf, sem = refs[sides + 2 :]
    count = own_buf.shape[0]
    features = sides * own_buf.shape[1]
    states = [[] for _ in range(sides)]
    for b in range(blocks):
        rows = [rows_refs[side * blocks + b][...].astype(jnp.float32) for side in range(sides)]
        row_sum = sum(jnp.sum(x, axis=1, keepdims=True) for x in rows)
        row_squares = sum(jnp.sum(x * x, axis=1, keepdims=True) for x in rows)
        mean = row_sum / features
        variance = row_squares / features - mean * mean
        scale = lax.rsqrt(variance + 1e-05)
        for side in range(sides):
            gate = gate_refs[side * blocks + b][...].astype(jnp.float32)
            states[side].append(((rows[side] - mean) * scale * gate).astype(jnp.bfloat16))
        if b == 0:
            own_buf[...] = states[0][0]
            keep = pltpu.make_async_copy(own_buf, states_ref, sem)
            keep.start()
    states = [jnp.concatenate(x, axis=0) for x in states]
    units = weight_refs[0].shape[1]
    step = min(256, units)
    total = jnp.zeros((count * blocks, LANES), jnp.float32)
    for first in range(0, units, step):
        cols = slice(first, first + step)
        act = bias_ref[:, cols]
        for side in range(sides):
            act = act + jnp.dot(
                states[side], weight_refs[side][:, cols], preferred_element_type=jnp.float32
            )
        half = 0.5 * act
        hidden = half * jnp.tanh(half) + half
        part = hidden * out_w_ref[:, cols]
        for lane in range(0, step, LANES):
            total = total + part[:, lane : lane + LANES]
    scores = jnp.sum(total.T, axis=0, keepdims=True)
    for b in range(blocks):
        score_refs[b][...] = scores[:, b * count : (b + 1) * count]
    keep.wait()


def local(
    sizes,
    queries,
    hist_keys,
    hist_values,
    cand_user,
    time_bucket,
    hist_len,
    cand_gate,
    time_bias,
    tower_in,
    tower_bias,
    tower_out,
):
    hists, towers, sides = sizes["hist"], sizes["tower"], sizes["head"]
    users, events, width = hist_keys.shape
    count = queries.shape[0]
    heads = width // DH
    features = width * sides
    f32, bf16 = jnp.float32, jnp.bfloat16

    owners = jnp.pad(cand_user.astype(bf16).reshape(1, count), ((0, 7), (0, width - count)))
    packed = jnp.concatenate([queries, owners], axis=0)
    blocks = [packed] + [fetch(packed, "hist", step, hists) for step in range(1, hists)]

    share_type = jax.ShapeDtypeStruct((count, width), bf16)
    bias = call(
        bias_body,
        jax.ShapeDtypeStruct((users * heads, events), f32),
        [SMEM, VMEM, VMEM],
        BIASCOST,
        users * heads * events * 4,
    )(hist_len, time_bucket, time_bias.T)

    def shares_of(group):
        return call(
            functools.partial(share_body, len(group)),
            [share_type] * len(group),
            [VMEM] * (len(group) + 3),
            SHARECOST * len(group) * count * users * events * width,
            4 * users * events * width,
        )(*group, hist_keys, hist_values, bias)

    shares = list(shares_of([packed]))
    remote = [(step, blocks[step]) for step in range(1, hists)]
    for group in GROUPS(remote):
        for (step, _), share in zip(group, shares_of([block for _, block in group])):
            shares.append(give(share, "hist", step, hists))

    total, sent = call(
        total_body,
        (jax.ShapeDtypeStruct((count, width), f32), share_type),
        [VMEM] * hists,
        8 * count * width,
        8 * count * width,
    )(*shares)

    def spread(x):
        near = [x] + [fetch(x, "tower", step, towers) for step in range(1, towers)]
        far = [fetch(y, "head", step, sides) for step in range(1, sides) for y in near]
        return near + far

    gates = spread(cand_gate)
    weights = [tower_in] + [fetch(tower_in, "head", step, sides) for step in range(1, sides)]
    rows = spread(sent)
    rows[0] = total
    units = tower_in.shape[1]
    cand_states, *scores = call(
        functools.partial(tower_body, towers, sides),
        (share_type,) + tuple(jax.ShapeDtypeStruct((1, count), f32) for _ in range(towers)),
        [VMEM] * (2 * towers * sides + sides + 2),
        2 * towers * count * features * units,
        2 * features * units,
        out_specs=(pl.BlockSpec(memory_space=pl.ANY),) + (VMEM,) * towers,
        scratch=[pltpu.VMEM((count, width), bf16), pltpu.SemaphoreType.DMA],
    )(*rows, *gates, *weights, tower_bias.reshape(1, -1), tower_out.reshape(1, -1))
    cand_scores = scores[0]
    for step in range(1, towers):
        cand_scores = cand_scores + give(scores[step], "tower", step, towers)
    return (cand_states, cand_scores.reshape(count))


def solution(mesh):
    return jax.shard_map(
        functools.partial(local, dict(mesh.shape)),
        mesh=mesh,
        in_specs=(
            P(("groups", "hist", "tower"), "head"),
            P("groups", "hist", "head"),
            P("groups", "hist", "head"),
            P(("groups", "hist", "tower")),
            P("groups", "hist"),
            P("groups"),
            P(("groups", "hist", "tower"), "head"),
            P(None, "head"),
            P("head", "tower"),
            P("tower"),
            P("tower"),
        ),
        out_specs=(P(("groups", "hist", "tower"), "head"), P(("groups", "hist", "tower"))),
        check_vma=False,
    )
```

```python
import functools

import jax
import jax.numpy as jnp
from jax import lax
from jax.experimental import pallas as pl
from jax.experimental.pallas import tpu as pltpu
from jax.sharding import PartitionSpec as P

DH = 128
LANES = 128
DEAD = -1e30
HBM = pl.BlockSpec(memory_space=pltpu.HBM)
VMEM = pl.BlockSpec(memory_space=pltpu.VMEM)
SMEM = pl.BlockSpec(memory_space=pltpu.SMEM)
LIMIT = 32 * 1024 * 1024


def partner(index, step, count):
    if count & (count - 1) == 0:
        return index ^ step
    return (index + step) % count


def fetch(x, axis, step, count):
    return lax.ppermute(x, axis, [(partner(i, step, count), i) for i in range(count)])


def give(x, axis, step, count):
    return lax.ppermute(x, axis, [(i, partner(i, step, count)) for i in range(count)])


def hbm(x):
    return pltpu.with_memory_space_constraint(x, pltpu.HBM)


def call(body, outs, specs, flops, nbytes, out_specs=None, scratch=(), limit=LIMIT):
    return pl.pallas_call(
        body,
        out_shape=outs,
        in_specs=specs,
        out_specs=out_specs or jax.tree.map(lambda _: VMEM, outs),
        scratch_shapes=scratch,
        compiler_params=pltpu.CompilerParams(vmem_limit_bytes=limit),
        cost_estimate=pl.CostEstimate(
            flops=flops, bytes_accessed=nbytes, transcendentals=0
        ),
    )


def event_bias(len_ref, bucket_ref, table_ref, out_ref):
    users, events = bucket_ref.shape
    heads, buckets = table_ref.shape
    table = table_ref[...] * 0.5
    high = table.astype(jnp.bfloat16)
    rest = table - high.astype(jnp.float32)
    middle = rest.astype(jnp.bfloat16)
    low = (rest - middle.astype(jnp.float32)).astype(jnp.bfloat16)
    position = lax.axis_index("hist") * events + lax.broadcasted_iota(
        jnp.int32, (heads, events), 1
    )
    bucket_ids = lax.broadcasted_iota(jnp.int32, (buckets, events), 0)
    for user in range(users):
        onehot = jnp.where(bucket_ids == bucket_ref[user : user + 1, :], 1.0, 0.0).astype(
            jnp.bfloat16
        )
        bias = sum(
            jnp.dot(piece, onehot, preferred_element_type=jnp.float32)
            for piece in (high, middle, low)
        )
        out_ref[user * heads : (user + 1) * heads, :] = jnp.where(
            position < len_ref[user], bias, DEAD
        )


def pack_body(q_ref, id_ref, out_ref, id_buf, sems):
    count, width = q_ref.shape
    copies = [
        pltpu.make_async_copy(id_ref, id_buf, sems.at[0]),
        pltpu.make_async_copy(q_ref, out_ref.at[pl.ds(0, count)], sems.at[1]),
    ]
    for copy in copies:
        copy.start()
    copies[0].wait()
    ids = id_buf[...].astype(jnp.float32)
    ids = jnp.concatenate([ids] * (width // count), axis=1)
    out_ref[count:, :] = jnp.broadcast_to(ids, (out_ref.shape[0] - count, width)).astype(
        jnp.bfloat16
    )
    copies[1].wait()


def own_body(
    packed_ref, k_ref, v_ref, bucket_ref, table_ref, len_ref,
    share_ref, bias_ref, k_out, v_out,
    bucket_buf, table_buf, len_buf, sems,
):
    pairs = [
        (bucket_ref, bucket_buf),
        (table_ref, table_buf),
        (len_ref, len_buf),
        (k_ref, k_out),
        (v_ref, v_out),
    ]
    copies = [pltpu.make_async_copy(a, b, sems.at[i]) for i, (a, b) in enumerate(pairs)]
    for copy in copies:
        copy.start()
    for copy in copies[:3]:
        copy.wait()
    event_bias(len_buf, bucket_buf, table_buf, bias_ref)
    for copy in copies[3:]:
        copy.wait()
    share_body(1, packed_ref, k_out, v_out, bias_ref, share_ref)


def share_body(blocks, *refs):
    packed_refs, (k_ref, v_ref, bias_ref), out_refs = (
        refs[:blocks],
        refs[blocks : blocks + 3],
        refs[blocks + 3 :],
    )
    users, events, width = k_ref.shape
    each = out_refs[0].shape[0]
    heads = width // DH
    half_scale = 0.5 * DH ** (-0.5)
    eighth = jnp.full((8, LANES), 0.125, jnp.bfloat16)
    owner = jnp.concatenate(
        [
            lax.dot_general(
                ref[each:, :LANES],
                eighth,
                (((0,), (0,)), ((), ())),
                preferred_element_type=jnp.float32,
            )[:each]
            for ref in packed_refs
        ],
        axis=0,
    )
    mine = [owner == float(user) for user in range(users)]
    half_mine = [owner.astype(jnp.bfloat16) == float(user) for user in range(users)]
    wide = [
        jnp.concatenate([owner] * (events // LANES), axis=1) == float(user)
        for user in range(users)
    ]
    columns = [slice(head * DH, (head + 1) * DH) for head in range(heads)]
    logits, weights = [], []
    for cols in columns:
        query = jnp.concatenate([ref[:each, cols] for ref in packed_refs], axis=0)
        query = jnp.concatenate(
            [jnp.where(mask, query, jnp.zeros_like(query)) for mask in half_mine], axis=1
        )
        keys = jnp.concatenate([k_ref[user, :, cols] for user in range(users)], axis=1)
        logits.append(
            lax.dot_general(
                query, keys, (((1,), (1,)), ((), ())), preferred_element_type=jnp.float32
            )
        )
    for head in range(heads):
        bias = jnp.broadcast_to(bias_ref[head : head + 1, :], logits[head].shape)
        for user in range(1, users):
            row = user * heads + head
            bias = jnp.where(wide[user], bias_ref[row : row + 1, :], bias)
        half = logits[head] * half_scale + bias
        weights.append((half * jnp.tanh(half) + half).astype(jnp.bfloat16))
    for head, cols in enumerate(columns):
        values = jnp.concatenate([v_ref[user, :, cols] for user in range(users)], axis=1)
        mixed = jnp.dot(weights[head], values, preferred_element_type=jnp.float32)
        share = mixed[:, :DH]
        for user in range(1, users):
            share = jnp.where(mine[user], mixed[:, user * DH : (user + 1) * DH], share)
        share = share.astype(jnp.bfloat16)
        for block, out_ref in enumerate(out_refs):
            out_ref[:, cols] = share[block * each : (block + 1) * each]


def total_body(*refs):
    *share_refs, total_ref, sent_ref = refs
    total = share_refs[0][...].astype(jnp.float32)
    for share_ref in share_refs[1:]:
        total = total + share_ref[...].astype(jnp.float32)
    total_ref[...] = total
    sent_ref[...] = total.astype(jnp.bfloat16)


def tower_body(blocks, sides, *refs):
    parts = blocks * sides
    rows_refs, gate_refs, refs = refs[:parts], refs[parts : 2 * parts], refs[2 * parts :]
    weight_refs = refs[:sides]
    bias_ref, out_w_ref = refs[sides], refs[sides + 1]
    states_ref, *score_refs, own_buf, sem = refs[sides + 2 :]
    count = own_buf.shape[0]
    features = sides * own_buf.shape[1]
    states = [[] for _ in range(sides)]
    for b in range(blocks):
        rows = [rows_refs[side * blocks + b][...].astype(jnp.float32) for side in range(sides)]
        row_sum = sum(jnp.sum(x, axis=1, keepdims=True) for x in rows)
        row_squares = sum(jnp.sum(x * x, axis=1, keepdims=True) for x in rows)
        mean = row_sum / features
        variance = row_squares / features - mean * mean
        scale = lax.rsqrt(variance + 1e-05)
        for side in range(sides):
            gate = gate_refs[side * blocks + b][...].astype(jnp.float32)
            states[side].append(((rows[side] - mean) * scale * gate).astype(jnp.bfloat16))
        if b == 0:
            own_buf[...] = states[0][0]
            keep = pltpu.make_async_copy(own_buf, states_ref, sem)
            keep.start()
    states = [jnp.concatenate(x, axis=0) for x in states]
    units = weight_refs[0].shape[1]
    step = min(256, units)
    total = jnp.zeros((count * blocks, LANES), jnp.float32)
    for first in range(0, units, step):
        cols = slice(first, first + step)
        act = bias_ref[:, cols]
        for side in range(sides):
            act = act + jnp.dot(
                states[side], weight_refs[side][:, cols], preferred_element_type=jnp.float32
            )
        half = 0.5 * act
        hidden = half * jnp.tanh(half) + half
        part = hidden * out_w_ref[:, cols]
        for lane in range(0, step, LANES):
            total = total + part[:, lane : lane + LANES]
    scores = jnp.sum(total.T, axis=0, keepdims=True)
    for b in range(blocks):
        score_refs[b][...] = scores[:, b * count : (b + 1) * count]
    keep.wait()


def local(
    sizes,
    queries,
    hist_keys,
    hist_values,
    cand_user,
    time_bucket,
    hist_len,
    cand_gate,
    time_bias,
    tower_in,
    tower_bias,
    tower_out,
):
    hists, towers, sides = sizes["hist"], sizes["tower"], sizes["head"]
    users, events, width = hist_keys.shape
    count = queries.shape[0]
    heads = width // DH
    features = width * sides
    f32, bf16 = jnp.float32, jnp.bfloat16

    packed = call(
        pack_body,
        pltpu.VMEM((count + 8, width), bf16),
        [HBM] * 2,
        0,
        4 * count * width,
        scratch=[pltpu.VMEM((1, count), jnp.int32), pltpu.SemaphoreType.DMA((2,))],
    )(hbm(queries), hbm(cand_user.reshape(1, count)))
    blocks = [packed] + [fetch(packed, "hist", step, hists) for step in range(1, hists)]

    share_type = pltpu.VMEM((count, width), bf16)
    own_share, bias, keys, values = call(
        own_body,
        (
            share_type,
            pltpu.VMEM((users * heads, events), f32),
            pltpu.VMEM(hist_keys.shape, bf16),
            pltpu.VMEM(hist_values.shape, bf16),
        ),
        [VMEM] + [HBM] * 5,
        0,
        4 * users * events * width,
        scratch=[
            pltpu.VMEM(time_bucket.shape, jnp.int32),
            pltpu.VMEM((heads, time_bias.shape[0]), f32),
            pltpu.SMEM(hist_len.shape, jnp.int32),
            pltpu.SemaphoreType.DMA((5,)),
        ],
    )(packed, *map(hbm, (hist_keys, hist_values, time_bucket, time_bias.T, hist_len)))

    def shares_of(group):
        return call(
            functools.partial(share_body, len(group)),
            [share_type] * len(group),
            [VMEM] * (len(group) + 3),
            0,
            4 * users * events * width,
        )(*group, keys, values, bias)

    shares = [own_share]
    for step in range(1, hists):
        (share,) = shares_of([blocks[step]])
        shares.append(give(share, "hist", step, hists))

    total, sent = call(
        total_body,
        (pltpu.VMEM((count, width), f32), share_type),
        [VMEM] * hists,
        8 * count * width,
        8 * count * width,
    )(*shares)

    def spread(x):
        near = [x] + [fetch(x, "tower", step, towers) for step in range(1, towers)]
        far = [fetch(y, "head", step, sides) for step in range(1, sides) for y in near]
        return near + far

    cand_gate, _ = lax.optimization_barrier((cand_gate, shares[-1]))
    gates = spread(cand_gate)
    weights = [tower_in] + [fetch(tower_in, "head", step, sides) for step in range(1, sides)]
    rows = spread(sent)
    rows[0] = total
    units = tower_in.shape[1]
    cand_states, *scores = call(
        functools.partial(tower_body, towers, sides),
        (jax.ShapeDtypeStruct((count, width), bf16),)
        + tuple(pltpu.VMEM((1, count), f32) for _ in range(towers)),
        [VMEM] * (2 * towers * sides + sides + 2),
        2 * towers * count * features * units,
        2 * features * units,
        out_specs=(pl.BlockSpec(memory_space=pl.ANY),) + (VMEM,) * towers,
        scratch=[pltpu.VMEM((count, width), bf16), pltpu.SemaphoreType.DMA],
    )(*rows, *gates, *weights, tower_bias.reshape(1, -1), tower_out.reshape(1, -1))
    cand_scores = scores[0]
    for step in range(1, towers):
        cand_scores = cand_scores + give(scores[step], "tower", step, towers)
    return (cand_states, cand_scores.reshape(count))


def solution(mesh):
    return jax.shard_map(
        functools.partial(local, dict(mesh.shape)),
        mesh=mesh,
        in_specs=(
            P(("groups", "hist", "tower"), "head"),
            P("groups", "hist", "head"),
            P("groups", "hist", "head"),
            P(("groups", "hist", "tower")),
            P("groups", "hist"),
            P("groups"),
            P(("groups", "hist", "tower"), "head"),
            P(None, "head"),
            P("head", "tower"),
            P("tower"),
            P("tower"),
        ),
        out_specs=(P(("groups", "hist", "tower"), "head"), P(("groups", "hist", "tower"))),
        check_vma=False,
    )
```

```python
import functools

import jax
import jax.numpy as jnp
from jax import lax
from jax.experimental import pallas as pl
from jax.experimental.pallas import tpu as pltpu
from jax.sharding import PartitionSpec as P

DH = 128
LANES = 128
DEAD = -1e30
HBM = pl.BlockSpec(memory_space=pltpu.HBM)
VMEM = pl.BlockSpec(memory_space=pltpu.VMEM)
SMEM = pl.BlockSpec(memory_space=pltpu.SMEM)
LIMIT = 32 * 1024 * 1024


def partner(index, step, count):
    if count & (count - 1) == 0:
        return index ^ step
    return (index + step) % count


def fetch(x, axis, step, count):
    return lax.ppermute(x, axis, [(partner(i, step, count), i) for i in range(count)])


def give(x, axis, step, count):
    return lax.ppermute(x, axis, [(i, partner(i, step, count)) for i in range(count)])


def hbm(x):
    return pltpu.with_memory_space_constraint(x, pltpu.HBM)


def call(body, outs, specs, flops, nbytes, out_specs=None, scratch=(), limit=LIMIT):
    return pl.pallas_call(
        body,
        out_shape=outs,
        in_specs=specs,
        out_specs=out_specs or jax.tree.map(lambda _: VMEM, outs),
        scratch_shapes=scratch,
        compiler_params=pltpu.CompilerParams(vmem_limit_bytes=limit),
        cost_estimate=pl.CostEstimate(
            flops=flops, bytes_accessed=nbytes, transcendentals=0
        ),
    )


def event_bias(len_ref, bucket_ref, table_ref, out_ref):
    users, events = bucket_ref.shape
    heads, buckets = table_ref.shape
    table = table_ref[...] * 0.5
    high = table.astype(jnp.bfloat16)
    rest = table - high.astype(jnp.float32)
    middle = rest.astype(jnp.bfloat16)
    low = (rest - middle.astype(jnp.float32)).astype(jnp.bfloat16)
    position = lax.axis_index("hist") * events + lax.broadcasted_iota(
        jnp.int32, (heads, events), 1
    )
    bucket_ids = lax.broadcasted_iota(jnp.int32, (buckets, events), 0)
    for user in range(users):
        onehot = jnp.where(bucket_ids == bucket_ref[user : user + 1, :], 1.0, 0.0).astype(
            jnp.bfloat16
        )
        bias = sum(
            jnp.dot(piece, onehot, preferred_element_type=jnp.float32)
            for piece in (high, middle, low)
        )
        out_ref[user * heads : (user + 1) * heads, :] = jnp.where(
            position < len_ref[user], bias, DEAD
        )


def pack_body(q_ref, id_ref, out_ref, id_buf, sems):
    count, width = q_ref.shape
    copies = [
        pltpu.make_async_copy(id_ref, id_buf, sems.at[0]),
        pltpu.make_async_copy(q_ref, out_ref.at[pl.ds(0, count)], sems.at[1]),
    ]
    for copy in copies:
        copy.start()
    copies[0].wait()
    ids = id_buf[...].astype(jnp.float32)
    ids = jnp.concatenate([ids] * (width // count), axis=1)
    out_ref[count:, :] = jnp.broadcast_to(ids, (out_ref.shape[0] - count, width)).astype(
        jnp.bfloat16
    )
    copies[1].wait()


def own_body(
    packed_ref, k_ref, v_ref, bucket_ref, table_ref, len_ref,
    share_ref, bias_ref, k_out, v_out,
    bucket_buf, table_buf, len_buf, sems,
):
    pairs = [
        (bucket_ref, bucket_buf),
        (table_ref, table_buf),
        (len_ref, len_buf),
        (k_ref, k_out),
        (v_ref, v_out),
    ]
    copies = [pltpu.make_async_copy(a, b, sems.at[i]) for i, (a, b) in enumerate(pairs)]
    for copy in copies:
        copy.start()
    for copy in copies[:3]:
        copy.wait()
    event_bias(len_buf, bucket_buf, table_buf, bias_ref)
    for copy in copies[3:]:
        copy.wait()
    share_body(1, packed_ref, k_out, v_out, bias_ref, share_ref)


def share_body(blocks, *refs):
    packed_refs, (k_ref, v_ref, bias_ref), out_refs = (
        refs[:blocks],
        refs[blocks : blocks + 3],
        refs[blocks + 3 :],
    )
    users, events, width = k_ref.shape
    each = out_refs[0].shape[0]
    heads = width // DH
    half_scale = 0.5 * DH ** (-0.5)
    eighth = jnp.full((8, LANES), 0.125, jnp.bfloat16)
    owner = jnp.concatenate(
        [
            lax.dot_general(
                ref[each:, :LANES],
                eighth,
                (((0,), (0,)), ((), ())),
                preferred_element_type=jnp.float32,
            )[:each]
            for ref in packed_refs
        ],
        axis=0,
    )
    mine = [owner == float(user) for user in range(users)]
    half_mine = [owner.astype(jnp.bfloat16) == float(user) for user in range(users)]
    wide = [
        jnp.concatenate([owner] * (events // LANES), axis=1) == float(user)
        for user in range(users)
    ]
    columns = [slice(head * DH, (head + 1) * DH) for head in range(heads)]
    logits, weights = [], []
    for cols in columns:
        query = jnp.concatenate([ref[:each, cols] for ref in packed_refs], axis=0)
        query = jnp.concatenate(
            [jnp.where(mask, query, jnp.zeros_like(query)) for mask in half_mine], axis=1
        )
        keys = jnp.concatenate([k_ref[user, :, cols] for user in range(users)], axis=1)
        logits.append(
            lax.dot_general(
                query, keys, (((1,), (1,)), ((), ())), preferred_element_type=jnp.float32
            )
        )
    for head in range(heads):
        bias = jnp.broadcast_to(bias_ref[head : head + 1, :], logits[head].shape)
        for user in range(1, users):
            row = user * heads + head
            bias = jnp.where(wide[user], bias_ref[row : row + 1, :], bias)
        half = logits[head] * half_scale + bias
        weights.append((half * jnp.tanh(half) + half).astype(jnp.bfloat16))
    for head, cols in enumerate(columns):
        values = jnp.concatenate([v_ref[user, :, cols] for user in range(users)], axis=1)
        mixed = jnp.dot(weights[head], values, preferred_element_type=jnp.float32)
        share = mixed[:, :DH]
        for user in range(1, users):
            share = jnp.where(mine[user], mixed[:, user * DH : (user + 1) * DH], share)
        share = share.astype(jnp.bfloat16)
        for block, out_ref in enumerate(out_refs):
            out_ref[:, cols] = share[block * each : (block + 1) * each]


def total_body(*refs):
    *share_refs, total_ref, sent_ref = refs
    total = share_refs[0][...].astype(jnp.float32)
    for share_ref in share_refs[1:]:
        total = total + share_ref[...].astype(jnp.float32)
    total_ref[...] = total
    sent_ref[...] = total.astype(jnp.bfloat16)


def silu_dot(act, out_w, total):
    half = 0.5 * act
    part = (half * jnp.tanh(half) + half) * out_w
    for lane in range(0, part.shape[1], LANES):
        total = total + part[:, lane : lane + LANES]
    return total


def chunks(units):
    step = min(256, units)
    return [slice(first, first + step) for first in range(0, units, step)]


def own_rows_body(sides, *refs):
    row_refs, gate_refs, weight_refs = refs[:sides], refs[sides : 2 * sides], refs[2 * sides : 3 * sides]
    bias_ref, out_w_ref, states_ref, score_ref, own_buf, sem = refs[3 * sides :]
    count = own_buf.shape[0]
    features = sides * own_buf.shape[1]
    rows = [ref[...].astype(jnp.float32) for ref in row_refs]
    mean = sum(jnp.sum(x, axis=1, keepdims=True) for x in rows) / features
    squares = sum(jnp.sum(x * x, axis=1, keepdims=True) for x in rows) / features
    scale = lax.rsqrt(squares - mean * mean + 1e-05)
    states = [
        ((x - mean) * scale * ref[...].astype(jnp.float32)).astype(jnp.bfloat16)
        for x, ref in zip(rows, gate_refs)
    ]
    own_buf[...] = states[0]
    keep = pltpu.make_async_copy(own_buf, states_ref, sem)
    keep.start()
    total = jnp.zeros((count, LANES), jnp.float32)
    for cols in chunks(weight_refs[0].shape[1]):
        act = bias_ref[:, cols]
        for x, ref in zip(states, weight_refs):
            act = act + jnp.dot(x, ref[:, cols], preferred_element_type=jnp.float32)
        total = silu_dot(act, out_w_ref[:, cols], total)
    score_ref[...] = jnp.sum(total.T, axis=0, keepdims=True)
    keep.wait()


def centred(row_refs, centre_refs):
    rows = jnp.concatenate([ref[...] for ref in row_refs], axis=0).astype(jnp.float32)
    near = jnp.concatenate([ref[...] for ref in centre_refs], axis=0).astype(jnp.float32)
    return rows - jnp.sum(near, axis=1, keepdims=True) / near.shape[1]


def gated(rows, gate_refs):
    gate = jnp.concatenate([ref[...] for ref in gate_refs], axis=0)
    rows = (rows * gate.astype(jnp.float32)).astype(jnp.bfloat16)
    return jnp.concatenate([rows, gate], axis=0)


def near_body(others, *refs):
    near_refs, gate_refs, (weight_ref, out_ref) = (
        refs[:others],
        refs[others : 2 * others],
        refs[2 * others :],
    )
    left = gated(centred(near_refs, near_refs), gate_refs)
    for cols in chunks(weight_ref.shape[1]):
        out_ref[:, cols] = jnp.dot(
            left, weight_ref[:, cols], preferred_element_type=jnp.float32
        )


def far_body(others, sides, *refs):
    near_refs, refs = refs[:others], refs[others:]
    far_refs, refs = refs[: others * (sides - 1)], refs[others * (sides - 1) :]
    gate_refs, refs = refs[: others * (sides - 1)], refs[others * (sides - 1) :]
    weight_refs, refs = refs[: sides - 1], refs[sides - 1 :]
    done_ref, bias_ref, out_w_ref, *score_refs = refs
    rows = [centred(near_refs, near_refs)]
    left = []
    for side in range(sides - 1):
        part = slice(side * others, (side + 1) * others)
        rows.append(centred(far_refs[part], near_refs))
        left.append(gated(rows[-1], gate_refs[part]))
    count, width = rows[0].shape
    mean = sum(jnp.sum(x, axis=1, keepdims=True) for x in rows) / (sides * width)
    squares = sum(jnp.sum(x * x, axis=1, keepdims=True) for x in rows) / (sides * width)
    scale = lax.rsqrt(squares - mean * mean + 1e-05)
    total = jnp.zeros((count, LANES), jnp.float32)
    for cols in chunks(weight_refs[0].shape[1]):
        act = done_ref[:, cols]
        for x, ref in zip(left, weight_refs):
            act = act + jnp.dot(x, ref[:, cols], preferred_element_type=jnp.float32)
        act = (act[:count] - mean * act[count:]) * scale + bias_ref[:, cols]
        total = silu_dot(act, out_w_ref[:, cols], total)
    scores = jnp.sum(total.T, axis=0, keepdims=True)
    each = near_refs[0].shape[0]
    for b, ref in enumerate(score_refs):
        ref[...] = scores[:, b * each : (b + 1) * each]


def local(
    sizes,
    queries,
    hist_keys,
    hist_values,
    cand_user,
    time_bucket,
    hist_len,
    cand_gate,
    time_bias,
    tower_in,
    tower_bias,
    tower_out,
):
    hists, towers, sides = sizes["hist"], sizes["tower"], sizes["head"]
    users, events, width = hist_keys.shape
    count = queries.shape[0]
    heads = width // DH
    features = width * sides
    f32, bf16 = jnp.float32, jnp.bfloat16

    packed = call(
        pack_body,
        pltpu.VMEM((count + 8, width), bf16),
        [HBM] * 2,
        0,
        4 * count * width,
        scratch=[pltpu.VMEM((1, count), jnp.int32), pltpu.SemaphoreType.DMA((2,))],
    )(hbm(queries), hbm(cand_user.reshape(1, count)))
    blocks = [packed] + [fetch(packed, "hist", step, hists) for step in range(1, hists)]

    share_type = pltpu.VMEM((count, width), bf16)
    own_share, bias, keys, values = call(
        own_body,
        (
            share_type,
            pltpu.VMEM((users * heads, events), f32),
            pltpu.VMEM(hist_keys.shape, bf16),
            pltpu.VMEM(hist_values.shape, bf16),
        ),
        [VMEM] + [HBM] * 5,
        0,
        4 * users * events * width,
        scratch=[
            pltpu.VMEM(time_bucket.shape, jnp.int32),
            pltpu.VMEM((heads, time_bias.shape[0]), f32),
            pltpu.SMEM(hist_len.shape, jnp.int32),
            pltpu.SemaphoreType.DMA((5,)),
        ],
    )(packed, *map(hbm, (hist_keys, hist_values, time_bucket, time_bias.T, hist_len)))

    def shares_of(group):
        return call(
            functools.partial(share_body, len(group)),
            [share_type] * len(group),
            [VMEM] * (len(group) + 3),
            0,
            4 * users * events * width,
        )(*group, keys, values, bias)

    shares = [own_share]
    for step in range(1, hists):
        (share,) = shares_of([blocks[step]])
        shares.append(give(share, "hist", step, hists))

    total, sent = call(
        total_body,
        (pltpu.VMEM((count, width), f32), share_type),
        [VMEM] * hists,
        8 * count * width,
        8 * count * width,
    )(*shares)

    def across(x):
        return [fetch(x, "tower", step, towers) for step in range(1, towers)]

    def sibling(blocks):
        return [fetch(x, "head", step, sides) for step in range(1, sides) for x in blocks]

    own_gate = cand_gate
    cand_gate, _ = lax.optimization_barrier((cand_gate, shares[-1]))
    near_gates = across(cand_gate)
    far_gates, own_gates = sibling(near_gates), [own_gate] + sibling([own_gate])
    weights = [tower_in] + [fetch(tower_in, "head", step, sides) for step in range(1, sides)]
    near, own_far = across(sent), sibling([sent])
    others, units = towers - 1, tower_in.shape[1]
    layer = (tower_bias.reshape(1, -1), tower_out.reshape(1, -1))
    score_type = pltpu.VMEM((1, count), f32)
    partial_type = pltpu.VMEM((2 * others * count, units), f32)
    cost = 2 * count * features * units
    cand_states, cand_scores = call(
        functools.partial(own_rows_body, sides),
        (jax.ShapeDtypeStruct((count, width), bf16), score_type),
        [VMEM] * (3 * sides + 2),
        cost,
        2 * features * units,
        out_specs=(HBM, VMEM),
        scratch=[pltpu.VMEM((count, width), bf16), pltpu.SemaphoreType.DMA],
    )(total, *own_far, *own_gates, *weights, *layer)
    near = [lax.optimization_barrier((x, cand_scores))[0] for x in near]
    far = sibling(near)
    near_part = call(
        functools.partial(near_body, others),
        partial_type,
        [VMEM] * (2 * others + 1),
        others * cost // sides,
        2 * features * units // sides,
    )(*near, *near_gates, weights[0])
    scores = call(
        functools.partial(far_body, others, sides),
        (score_type,) * others,
        [VMEM] * (others * (2 * sides - 1) + sides + 2),
        others * cost,
        2 * features * units,
    )(*near, *far, *far_gates, *weights[1:], near_part, *layer)
    for step in range(1, towers):
        cand_scores = cand_scores + give(scores[step - 1], "tower", step, towers)
    return (cand_states, cand_scores.reshape(count))


def solution(mesh):
    return jax.shard_map(
        functools.partial(local, dict(mesh.shape)),
        mesh=mesh,
        in_specs=(
            P(("groups", "hist", "tower"), "head"),
            P("groups", "hist", "head"),
            P("groups", "hist", "head"),
            P(("groups", "hist", "tower")),
            P("groups", "hist"),
            P("groups"),
            P(("groups", "hist", "tower"), "head"),
            P(None, "head"),
            P("head", "tower"),
            P("tower"),
            P("tower"),
        ),
        out_specs=(P(("groups", "hist", "tower"), "head"), P(("groups", "hist", "tower"))),
        check_vma=False,
    )
```

```python
import functools

import jax
import jax.numpy as jnp
from jax import lax
from jax.experimental import pallas as pl
from jax.experimental.pallas import tpu as pltpu
from jax.sharding import PartitionSpec as P

DH = 128
LANES = 128
DEAD = -1e30
HBM = pl.BlockSpec(memory_space=pltpu.HBM)
VMEM = pl.BlockSpec(memory_space=pltpu.VMEM)
SMEM = pl.BlockSpec(memory_space=pltpu.SMEM)
LIMIT = 32 * 1024 * 1024


def partner(index, step, count):
    if count & (count - 1) == 0:
        return index ^ step
    return (index + step) % count


def fetch(x, axis, step, count):
    return lax.ppermute(x, axis, [(partner(i, step, count), i) for i in range(count)])


def give(x, axis, step, count):
    return lax.ppermute(x, axis, [(i, partner(i, step, count)) for i in range(count)])


def hbm(x):
    return pltpu.with_memory_space_constraint(x, pltpu.HBM)


def call(body, outs, specs, flops, nbytes, out_specs=None, scratch=(), limit=LIMIT):
    return pl.pallas_call(
        body,
        out_shape=outs,
        in_specs=specs,
        out_specs=out_specs or jax.tree.map(lambda _: VMEM, outs),
        scratch_shapes=scratch,
        compiler_params=pltpu.CompilerParams(vmem_limit_bytes=limit),
        cost_estimate=pl.CostEstimate(
            flops=flops, bytes_accessed=nbytes, transcendentals=0
        ),
    )


def event_bias(len_ref, bucket_ref, table_ref, out_ref):
    users, events = bucket_ref.shape
    heads, buckets = table_ref.shape
    table = table_ref[...] * 0.5
    high = table.astype(jnp.bfloat16)
    rest = table - high.astype(jnp.float32)
    middle = rest.astype(jnp.bfloat16)
    low = (rest - middle.astype(jnp.float32)).astype(jnp.bfloat16)
    position = lax.axis_index("hist") * events + lax.broadcasted_iota(
        jnp.int32, (heads, events), 1
    )
    bucket_ids = lax.broadcasted_iota(jnp.int32, (buckets, events), 0)
    for user in range(users):
        onehot = jnp.where(bucket_ids == bucket_ref[user : user + 1, :], 1.0, 0.0).astype(
            jnp.bfloat16
        )
        bias = sum(
            jnp.dot(piece, onehot, preferred_element_type=jnp.float32)
            for piece in (high, middle, low)
        )
        out_ref[user * heads : (user + 1) * heads, :] = jnp.where(
            position < len_ref[user], bias, DEAD
        )


def pack_body(q_ref, id_ref, out_ref, id_buf, sems):
    count, width = q_ref.shape
    copies = [
        pltpu.make_async_copy(id_ref, id_buf, sems.at[0]),
        pltpu.make_async_copy(q_ref, out_ref.at[pl.ds(0, count)], sems.at[1]),
    ]
    for copy in copies:
        copy.start()
    copies[0].wait()
    ids = id_buf[...].astype(jnp.float32)
    ids = jnp.concatenate([ids] * (width // count), axis=1)
    out_ref[count:, :] = jnp.broadcast_to(ids, (out_ref.shape[0] - count, width)).astype(
        jnp.bfloat16
    )
    copies[1].wait()


def load_body(
    k_ref, v_ref, bucket_ref, table_ref, len_ref,
    bias_ref, k_out, v_out,
    bucket_buf, table_buf, len_buf, sems,
):
    pairs = [
        (bucket_ref, bucket_buf),
        (table_ref, table_buf),
        (len_ref, len_buf),
        (k_ref, k_out),
        (v_ref, v_out),
    ]
    copies = [pltpu.make_async_copy(a, b, sems.at[i]) for i, (a, b) in enumerate(pairs)]
    for copy in copies:
        copy.start()
    for copy in copies[:3]:
        copy.wait()
    event_bias(len_buf, bucket_buf, table_buf, bias_ref)
    for copy in copies[3:]:
        copy.wait()


def share_body(blocks, *refs):
    packed_refs, (k_ref, v_ref, bias_ref), out_refs = (
        refs[:blocks],
        refs[blocks : blocks + 3],
        refs[blocks + 3 :],
    )
    users, events, width = k_ref.shape
    each = out_refs[0].shape[0]
    heads = width // DH
    half_scale = 0.5 * DH ** (-0.5)
    eighth = jnp.full((8, LANES), 0.125, jnp.bfloat16)
    owner = jnp.concatenate(
        [
            lax.dot_general(
                ref[each:, :LANES],
                eighth,
                (((0,), (0,)), ((), ())),
                preferred_element_type=jnp.float32,
            )[:each]
            for ref in packed_refs
        ],
        axis=0,
    )
    mine = [owner == float(user) for user in range(users)]
    half_mine = [owner.astype(jnp.bfloat16) == float(user) for user in range(users)]
    wide = [
        jnp.concatenate([owner] * (events // LANES), axis=1) == float(user)
        for user in range(users)
    ]
    columns = [slice(head * DH, (head + 1) * DH) for head in range(heads)]
    logits, weights = [], []
    for cols in columns:
        query = jnp.concatenate([ref[:each, cols] for ref in packed_refs], axis=0)
        query = jnp.concatenate(
            [jnp.where(mask, query, jnp.zeros_like(query)) for mask in half_mine], axis=1
        )
        keys = jnp.concatenate([k_ref[user, :, cols] for user in range(users)], axis=1)
        logits.append(
            lax.dot_general(
                query, keys, (((1,), (1,)), ((), ())), preferred_element_type=jnp.float32
            )
        )
    for head in range(heads):
        bias = jnp.broadcast_to(bias_ref[head : head + 1, :], logits[head].shape)
        for user in range(1, users):
            row = user * heads + head
            bias = jnp.where(wide[user], bias_ref[row : row + 1, :], bias)
        half = logits[head] * half_scale + bias
        weights.append((half * jnp.tanh(half) + half).astype(jnp.bfloat16))
    for head, cols in enumerate(columns):
        values = jnp.concatenate([v_ref[user, :, cols] for user in range(users)], axis=1)
        mixed = jnp.dot(weights[head], values, preferred_element_type=jnp.float32)
        share = mixed[:, :DH]
        for user in range(1, users):
            share = jnp.where(mine[user], mixed[:, user * DH : (user + 1) * DH], share)
        share = share.astype(jnp.bfloat16)
        for block, out_ref in enumerate(out_refs):
            out_ref[:, cols] = share[block * each : (block + 1) * each]


def total_body(*refs):
    *share_refs, total_ref, sent_ref = refs
    total = share_refs[0][...].astype(jnp.float32)
    for share_ref in share_refs[1:]:
        total = total + share_ref[...].astype(jnp.float32)
    total_ref[...] = total
    sent_ref[...] = total.astype(jnp.bfloat16)


def silu_dot(act, out_w, total):
    half = 0.5 * act
    part = (half * jnp.tanh(half) + half) * out_w
    for lane in range(0, part.shape[1], LANES):
        total = total + part[:, lane : lane + LANES]
    return total


def chunks(units):
    step = min(256, units)
    return [slice(first, first + step) for first in range(0, units, step)]


def own_rows_body(sides, *refs):
    row_refs, gate_refs, weight_refs = refs[:sides], refs[sides : 2 * sides], refs[2 * sides : 3 * sides]
    bias_ref, out_w_ref, states_ref, score_ref, own_buf, sem = refs[3 * sides :]
    count = own_buf.shape[0]
    features = sides * own_buf.shape[1]
    rows = [ref[...].astype(jnp.float32) for ref in row_refs]
    mean = sum(jnp.sum(x, axis=1, keepdims=True) for x in rows) / features
    squares = sum(jnp.sum(x * x, axis=1, keepdims=True) for x in rows) / features
    scale = lax.rsqrt(squares - mean * mean + 1e-05)
    states = [
        ((x - mean) * scale * ref[...].astype(jnp.float32)).astype(jnp.bfloat16)
        for x, ref in zip(rows, gate_refs)
    ]
    own_buf[...] = states[0]
    keep = pltpu.make_async_copy(own_buf, states_ref, sem)
    keep.start()
    total = jnp.zeros((count, LANES), jnp.float32)
    for cols in chunks(weight_refs[0].shape[1]):
        act = bias_ref[:, cols]
        for x, ref in zip(states, weight_refs):
            act = act + jnp.dot(x, ref[:, cols], preferred_element_type=jnp.float32)
        total = silu_dot(act, out_w_ref[:, cols], total)
    score_ref[...] = jnp.sum(total.T, axis=0, keepdims=True)
    keep.wait()


def centred(row_refs, centre_refs):
    rows = jnp.concatenate([ref[...] for ref in row_refs], axis=0).astype(jnp.float32)
    near = jnp.concatenate([ref[...] for ref in centre_refs], axis=0).astype(jnp.float32)
    return rows - jnp.sum(near, axis=1, keepdims=True) / near.shape[1]


def gated(rows, gate_refs):
    gate = jnp.concatenate([ref[...] for ref in gate_refs], axis=0)
    rows = (rows * gate.astype(jnp.float32)).astype(jnp.bfloat16)
    return jnp.concatenate([rows, gate], axis=0)


def near_body(others, *refs):
    near_refs, gate_refs, (weight_ref, out_ref) = (
        refs[:others],
        refs[others : 2 * others],
        refs[2 * others :],
    )
    left = gated(centred(near_refs, near_refs), gate_refs)
    for cols in chunks(weight_ref.shape[1]):
        out_ref[:, cols] = jnp.dot(
            left, weight_ref[:, cols], preferred_element_type=jnp.float32
        )


def far_body(others, sides, *refs):
    near_refs, refs = refs[:others], refs[others:]
    far_refs, refs = refs[: others * (sides - 1)], refs[others * (sides - 1) :]
    gate_refs, refs = refs[: others * (sides - 1)], refs[others * (sides - 1) :]
    weight_refs, refs = refs[: sides - 1], refs[sides - 1 :]
    done_ref, bias_ref, out_w_ref, *score_refs = refs
    rows = [centred(near_refs, near_refs)]
    left = []
    for side in range(sides - 1):
        part = slice(side * others, (side + 1) * others)
        rows.append(centred(far_refs[part], near_refs))
        left.append(gated(rows[-1], gate_refs[part]))
    count, width = rows[0].shape
    mean = sum(jnp.sum(x, axis=1, keepdims=True) for x in rows) / (sides * width)
    squares = sum(jnp.sum(x * x, axis=1, keepdims=True) for x in rows) / (sides * width)
    scale = lax.rsqrt(squares - mean * mean + 1e-05)
    total = jnp.zeros((count, LANES), jnp.float32)
    for cols in chunks(weight_refs[0].shape[1]):
        act = done_ref[:, cols]
        for x, ref in zip(left, weight_refs):
            act = act + jnp.dot(x, ref[:, cols], preferred_element_type=jnp.float32)
        act = (act[:count] - mean * act[count:]) * scale + bias_ref[:, cols]
        total = silu_dot(act, out_w_ref[:, cols], total)
    scores = jnp.sum(total.T, axis=0, keepdims=True)
    each = near_refs[0].shape[0]
    for b, ref in enumerate(score_refs):
        ref[...] = scores[:, b * each : (b + 1) * each]


def local(
    sizes,
    queries,
    hist_keys,
    hist_values,
    cand_user,
    time_bucket,
    hist_len,
    cand_gate,
    time_bias,
    tower_in,
    tower_bias,
    tower_out,
):
    hists, towers, sides = sizes["hist"], sizes["tower"], sizes["head"]
    users, events, width = hist_keys.shape
    count = queries.shape[0]
    heads = width // DH
    features = width * sides
    f32, bf16 = jnp.float32, jnp.bfloat16

    packed = call(
        pack_body,
        pltpu.VMEM((count + 8, width), bf16),
        [HBM] * 2,
        0,
        4 * count * width,
        scratch=[pltpu.VMEM((1, count), jnp.int32), pltpu.SemaphoreType.DMA((2,))],
    )(hbm(queries), hbm(cand_user.reshape(1, count)))
    blocks = [packed] + [fetch(packed, "hist", step, hists) for step in range(1, hists)]

    share_type = pltpu.VMEM((count, width), bf16)
    tied, _ = lax.optimization_barrier((hist_len, packed))
    bias, keys, values = call(
        load_body,
        (
            pltpu.VMEM((users * heads, events), f32),
            pltpu.VMEM(hist_keys.shape, bf16),
            pltpu.VMEM(hist_values.shape, bf16),
        ),
        [HBM] * 5,
        0,
        4 * users * events * width,
        scratch=[
            pltpu.VMEM(time_bucket.shape, jnp.int32),
            pltpu.VMEM((heads, time_bias.shape[0]), f32),
            pltpu.SMEM(hist_len.shape, jnp.int32),
            pltpu.SemaphoreType.DMA((5,)),
        ],
    )(*map(hbm, (hist_keys, hist_values, time_bucket, time_bias.T, tied)))

    def shares_of(group):
        return call(
            functools.partial(share_body, len(group)),
            [share_type] * len(group),
            [VMEM] * (len(group) + 3),
            0,
            4 * users * events * width,
        )(*group, keys, values, bias)

    shares = list(shares_of([packed]))
    for step in range(1, hists):
        (share,) = shares_of([blocks[step]])
        shares.append(give(share, "hist", step, hists))

    total, sent = call(
        total_body,
        (pltpu.VMEM((count, width), f32), share_type),
        [VMEM] * hists,
        8 * count * width,
        8 * count * width,
    )(*shares)

    def across(x):
        return [fetch(x, "tower", step, towers) for step in range(1, towers)]

    def sibling(blocks):
        return [fetch(x, "head", step, sides) for step in range(1, sides) for x in blocks]

    own_gate = cand_gate
    cand_gate, _ = lax.optimization_barrier((cand_gate, shares[-1]))
    near_gates = across(cand_gate)
    far_gates, own_gates = sibling(near_gates), [own_gate] + sibling([own_gate])
    weights = [tower_in] + [fetch(tower_in, "head", step, sides) for step in range(1, sides)]
    near, own_far = across(sent), sibling([sent])
    others, units = towers - 1, tower_in.shape[1]
    layer = (tower_bias.reshape(1, -1), tower_out.reshape(1, -1))
    score_type = pltpu.VMEM((1, count), f32)
    partial_type = pltpu.VMEM((2 * others * count, units), f32)
    cost = 2 * count * features * units
    cand_states, cand_scores = call(
        functools.partial(own_rows_body, sides),
        (jax.ShapeDtypeStruct((count, width), bf16), score_type),
        [VMEM] * (3 * sides + 2),
        cost,
        2 * features * units,
        out_specs=(HBM, VMEM),
        scratch=[pltpu.VMEM((count, width), bf16), pltpu.SemaphoreType.DMA],
    )(total, *own_far, *own_gates, *weights, *layer)
    near = [lax.optimization_barrier((x, cand_scores))[0] for x in near]
    far = sibling(near)
    near_part = call(
        functools.partial(near_body, others),
        partial_type,
        [VMEM] * (2 * others + 1),
        others * cost // sides,
        2 * features * units // sides,
    )(*near, *near_gates, weights[0])
    scores = call(
        functools.partial(far_body, others, sides),
        (score_type,) * others,
        [VMEM] * (others * (2 * sides - 1) + sides + 2),
        others * cost,
        2 * features * units,
    )(*near, *far, *far_gates, *weights[1:], near_part, *layer)
    for step in range(1, towers):
        cand_scores = cand_scores + give(scores[step - 1], "tower", step, towers)
    return (cand_states, cand_scores.reshape(count))


def solution(mesh):
    return jax.shard_map(
        functools.partial(local, dict(mesh.shape)),
        mesh=mesh,
        in_specs=(
            P(("groups", "hist", "tower"), "head"),
            P("groups", "hist", "head"),
            P("groups", "hist", "head"),
            P(("groups", "hist", "tower")),
            P("groups", "hist"),
            P("groups"),
            P(("groups", "hist", "tower"), "head"),
            P(None, "head"),
            P("head", "tower"),
            P("tower"),
            P("tower"),
        ),
        out_specs=(P(("groups", "hist", "tower"), "head"), P(("groups", "hist", "tower"))),
        check_vma=False,
    )
```
